1024 devices in a mesh: dp: 32 (over z_hi, x, core), tensor: 32 (over y, z_lo).
Axes of the slice: x: 4, y: 4, z: 32 (z_hi: 4, z_lo: 8; z = z_hi * 8 + z_lo), core: 2. Of those that a mesh axis runs over, the one named last changes fastest.
Arguments:
- hidden: bfloat16 [6144, 14336], P('dp', 'tensor'), parts along dimension 0, may hold values from -6 to 6
- down_weight: bfloat16 [14336, 8192], P('tensor'), may hold values from -0.046875 to 0.046875
- residual: bfloat16 [6144, 8192], P('dp', 'tensor'), parts along dimension 0, may hold values from -100 to 100
- norm_gain: float32 [8192], replicated, may hold values from 0.1 to 1.9
- qkv_weight: bfloat16 [8192, 5120], P(None, 'tensor'), may hold values from -0.0625 to 0.0625
Outputs:
- stream: bfloat16 [6144, 8192], P('dp', 'tensor'), parts along dimension 0
- qkv: bfloat16 [6144, 5120], P('dp', 'tensor'), parts along dimension 0
The draws below stay inside these ranges and needn't reach their ends.
There are 32 independent parts, one for each index of `dp`. The reference program is written for one: setup_inputs(seed, part) draws one part's arguments, and reference() takes and returns one part's arrays. A program takes and returns all parts, laid end to end along the dimension named above; an argument that names none is the same for every part. Nothing has to cross between parts.
All inputs are finite; a program needn't handle non-finite values.
Results may differ from the reference program's by a relative error of at most 0.02.
Values may be sent and summed in bfloat16 or wider, within the bound.
A program may use at most 64 MiB of HBM per device.

```python
import jax
import jax.numpy as jnp
from jax import lax

D = 8192
FF = 14336
QKV = 5120
TOKENS = 192
N_TENSOR = 32


def draw_residual(key, part):
    key_base, key_rows, key_cols = jax.random.split(jax.random.fold_in(key, 7), 3)
    values = jnp.clip(jax.random.normal(key_base, (TOKENS, D), jnp.float32), -4.0, 4.0)
    row_draw = jax.random.uniform(key_rows, (TOKENS, 1), jnp.float32)
    col_draw = jax.random.uniform(key_cols, (1, D), jnp.float32)
    position = jnp.arange(D, dtype=jnp.float32)[None, :] / D
    col_scale = jnp.power(3.0, position - 0.5) * jnp.power(10.0, 0.5 * (col_draw - 0.5))
    row_scale = jnp.power(10.0, row_draw - 0.5)
    return (values * row_scale * col_scale).astype(jnp.bfloat16)


def levels(rng, extent, shards, low, high):
    gain, own = 1.0, jax.random.fold_in(rng, 6)
    for dim, parts in shards:
        draws = jnp.exp(jax.random.uniform(jax.random.fold_in(own, dim), (parts,), jnp.float32, low / len(shards), high / len(shards)))
        gain = gain * jnp.repeat(draws, extent[dim] // parts).reshape([-1 if axis == dim else 1 for axis in range(len(extent))])
    return gain


def scatter_about(key, extent, spread, most, cuts=(), kind=jnp.bfloat16):
    loudness = levels(key, extent, cuts, -0.22, 0.18) if cuts else 1.0
    array = jax.random.normal(key, extent, jnp.float32) * spread * loudness
    return jnp.minimum(jnp.maximum(array, -most), most).astype(kind)


def setup_inputs(seed: int = 0, part: int = 0) -> dict:
    streams_of = jax.random.split(jax.random.key(seed), 6)
    part_splits = jax.random.split(jax.random.fold_in(streams_of[5], part), 6)
    hidden = scatter_about(part_splits[0], (TOKENS, FF), 1.0, 6.0, ((1, 32),))
    down_weight = scatter_about(streams_of[1], (FF, D), FF ** -0.5, 0.046875, ((0, 32),))
    residual = draw_residual(jax.random.fold_in(jax.random.fold_in(streams_of[5], part), 71), part)
    norm_gain = jnp.clip(1.0 + 0.18 * jax.random.normal(streams_of[3], (D,), jnp.float32), 0.1, 1.9)
    qkv_weight = scatter_about(streams_of[4], (D, QKV), D ** -0.5, 0.0625, ((1, 32),))
    return {"hidden": hidden, "down_weight": down_weight, "residual": residual, "norm_gain": norm_gain, "qkv_weight": qkv_weight}


epsilon = 1e-05

def reference(hidden, down_weight, residual, norm_gain, qkv_weight):
    groups = N_TENSOR
    width = FF // groups
    hidden_groups = jnp.transpose(hidden.reshape(TOKENS, groups, width), (1, 0, 2))
    down_groups = down_weight.reshape(groups, width, D)

    def add_group(total, pieces):
        part = jnp.dot(pieces[0], pieces[1], preferred_element_type=jnp.float32)
        part = lax.optimization_barrier(part.astype(jnp.bfloat16))
        return (total + part.astype(jnp.float32), None)
    start_total = jnp.zeros((TOKENS, D), jnp.float32)
    partial_sum, _ = lax.scan(add_group, start_total, (hidden_groups, down_groups))
    summed = partial_sum + residual.astype(jnp.float32)
    stream = summed.astype(jnp.bfloat16)
    scale = jnp.sqrt(lax.optimization_barrier(jnp.mean(summed * summed, axis=1, keepdims=True)) + epsilon)
    normed = (summed / scale * norm_gain[None, :]).astype(jnp.bfloat16)
    qkv = jnp.dot(normed, qkv_weight, preferred_element_type=jnp.float32).astype(jnp.bfloat16)
    return (stream, qkv)
```

```python
import jax
import jax.numpy as jnp
from jax import lax
from jax.experimental import pallas as pl
from jax.experimental.pallas import tpu as pltpu
from jax.sharding import PartitionSpec as P

EPS = 1e-05
T = 192
W = 256
NQ = 160
D = 8192
FG = 448
CHUNKS = ((0, 64), (64, 64), (128, 64))
NC = len(CHUNKS)
F32 = jnp.float32
BF16 = jnp.bfloat16
MESH = pl.DeviceIdType.MESH


def times_t(a, b):
    return lax.dot_general(a, b, (((1,), (1,)), ((), ())), preferred_element_type=F32)


def kernel(
    hid_hbm, wd_hbm, res_hbm, gain_hbm, wq_hbm,
    stream_ref, qkv_ref,
    hid, wd, res, gain, wq,
    wq0, part, y2a, y2b, y3l, y3r,
    s, zr, agg, aggs, zx, sg, acc, fs, fr,
    lsem, wsem,
    y1s, y1r, y2s, y2r, y3s, y3r_sem,
    z1s, z1r, z2s, z2r, gs, gr, fss, frs,
    q1s, q1r, q2s, q2r,
):
    t = lax.axis_index("tensor")
    dp = lax.axis_index("dp")
    y = t // 8
    z = t % 8
    h = z // 4
    l = z % 4
    rep = dp % 8
    dpb = dp - rep

    def at_y(k):
        return {"tensor": ((y + k) % 4) * 8 + z}

    def quad_l(m):
        lo = l % 2
        hi = l // 2
        if m % 2:
            lo = 1 - lo
        if m // 2:
            hi = 1 - hi
        return hi * 2 + lo

    def at_quad(m):
        return {"tensor": y * 8 + h * 4 + quad_l(m)}

    at_half = {"tensor": y * 8 + (1 - h) * 4 + l}

    def at_rep(m):
        return {"dp": dpb + (rep + m) % 8}

    right, left, across = at_y(1), at_y(3), at_y(2)
    peers = [right, left, across, at_half]
    peers += [at_quad(m) for m in (1, 2, 3)]
    peers += [at_rep(m) for m in range(1, 8)]

    def wd_copy(k):
        col = pl.multiple_of(((y + k) % 4) * 2048, 2048)
        return pltpu.make_async_copy(wd_hbm.at[:, pl.ds(col, 2048)], wd.at[k], wsem.at[k])

    c_hid = pltpu.make_async_copy(hid_hbm, hid, lsem.at[0])
    c_res = pltpu.make_async_copy(res_hbm, res, lsem.at[1])
    c_gain = pltpu.make_async_copy(gain_hbm, gain, lsem.at[2])
    own = pl.multiple_of(y * 2048, 2048)
    c_wq = pltpu.make_async_copy(wq_hbm.at[:, pl.ds(own, 2048)], wq0, lsem.at[3])
    c_hid.start()
    wd_copy(2).start()

    barrier = pltpu.get_barrier_semaphore()
    for p in peers:
        pl.semaphore_signal(barrier, 1, device_id=p, device_id_type=MESH)

    wd_copy(1).start()
    wd_copy(3).start()
    wd_copy(0).start()
    c_wq.start()
    c_res.start()
    c_gain.start()

    def remote(src, dst, ss, rs, dev):
        return pltpu.make_async_remote_copy(
            src_ref=src, dst_ref=dst, send_sem=ss, recv_sem=rs, device_id=dev, device_id_type=MESH
        )

    def matmul(k):
        wd_copy(k).wait()

        def body(j, c):
            cols = pl.ds(pl.multiple_of(j * W, W), W)
            part[k, j] = jnp.dot(hid[...], wd[k, :, cols], preferred_element_type=F32).astype(BF16)
            return c

        lax.fori_loop(0, 8, body, 0)

    def tok(c):
        return pl.ds(CHUNKS[c][0], CHUNKS[c][1])

    LO, HI = pl.ds(0, 4), pl.ds(4, 4)

    def wq_cols(owner):
        return pl.ds(pl.multiple_of(owner * 2048 + rep * W, W), W)

    def q1(k):
        src = wq_hbm.at[:, wq_cols((y + k) % 4)]
        return remote(src, wq.at[rep, 3 - k], q1s.at[k - 1], q1r.at[3 - k], at_y(k))

    def q1_recv(k):
        src = wq_hbm.at[:, wq_cols(y)]
        return remote(src, wq.at[rep, k - 1], q1s.at[3 - k], q1r.at[k - 1], at_y(k))

    def q2(m):
        blk = wq.at[rep]
        return remote(blk, blk, q2s.at[m - 1], q2r.at[m - 1], at_rep(m))

    def q2_recv(m):
        blk = wq.at[(rep + 8 - m) % 8]
        return remote(blk, blk, q2s.at[m - 1], q2r.at[m - 1], at_rep(m))

    def y1(c):
        return (
            remote(part.at[2, LO, tok(c)], y2a.at[:, tok(c)], y1s.at[0, c], y1r.at[0, c], right),
            remote(part.at[2, HI, tok(c)], y2b.at[:, tok(c)], y1s.at[1, c], y1r.at[1, c], left),
        )

    def y2(c):
        return (
            remote(part.at[1, HI, tok(c)], y3l.at[HI, tok(c)], y2s.at[0, c], y2r.at[0, c], right),
            remote(part.at[3, LO, tok(c)], y3r.at[LO, tok(c)], y2s.at[1, c], y2r.at[1, c], left),
        )

    def y3(c):
        return (
            remote(y2a.at[:, tok(c)], y3l.at[LO, tok(c)], y3s.at[0, c], y3r_sem.at[0, c], right),
            remote(y2b.at[:, tok(c)], y3r.at[HI, tok(c)], y3s.at[1, c], y3r_sem.at[1, c], left),
        )

    def start(ds):
        for d in ds:
            d.start()

    def aug(c):
        ra, rb = y1(c)
        ra.wait_recv()

        def body_a(j, x):
            y2a[j, tok(c)] = (y2a[j, tok(c)].astype(F32) + part[1, j, tok(c)].astype(F32)).astype(BF16)
            return x

        lax.fori_loop(0, 4, body_a, 0)
        y3(c)[0].start()
        rb.wait_recv()

        def body_b(j, x):
            y2b[j, tok(c)] = (y2b[j, tok(c)].astype(F32) + part[3, 4 + j, tok(c)].astype(F32)).astype(BF16)
            return x

        lax.fori_loop(0, 4, body_b, 0)
        y3(c)[1].start()

    def z1(c, m):
        dst = quad_l(m)
        return remote(s.at[:, dst, tok(c)], zr.at[m - 1, :, tok(c)], z1s.at[m - 1, c], z1r.at[m - 1, c], at_quad(m))

    def ysum(c):
        for d in y2(c) + y3(c):
            d.wait_recv()

        def body(j, x):
            v = part[0, j, tok(c)].astype(F32) + y3l[j, tok(c)].astype(F32) + y3r[j, tok(c)].astype(F32)
            s[j // 4, j % 4, tok(c)] = v.astype(BF16)
            return x

        lax.fori_loop(0, 8, body, 0)
        for m in (3, 2, 1):
            z1(c, m).start()

    def z2(c):
        return remote(aggs.at[:, tok(c)], zx.at[:, tok(c)], z2s.at[c], z2r.at[c], at_half)

    def zsum(c):
        for m in (1, 2, 3):
            z1(c, m).wait_recv()

        def body(hh, x):
            v = s[hh, l, tok(c)].astype(F32) + zr[0, hh, tok(c)].astype(F32)
            v = v + zr[1, hh, tok(c)].astype(F32) + zr[2, hh, tok(c)].astype(F32)
            mine = jnp.where(hh == h, 1.0, 0.0).astype(F32)
            v = v + res[tok(c)].astype(F32) * mine
            agg[hh, tok(c)] = v
            aggs[hh, tok(c)] = v.astype(BF16)
            return x

        lax.fori_loop(0, 2, body, 0)
        z2(c).start()

    def g(c, m):
        blk = sg.at[:, l, tok(c)]
        return remote(blk, blk, gs.at[m - 1, c], gr.at[m - 1, c], at_quad(m))

    def g_recv(c, m):
        blk = sg.at[:, quad_l(m), tok(c)]
        return remote(blk, blk, gs.at[m - 1, c], gr.at[m - 1, c], at_quad(m))

    def gather(c):
        z2(c).wait_recv()

        def body(hh, x):
            v = agg[hh, tok(c)] + zx[hh, tok(c)].astype(F32)
            sg[hh, l, tok(c)] = v.astype(BF16)
            return x

        lax.fori_loop(0, 2, body, 0)
        for m in (3, 2, 1):
            g(c, m).start()
        stream_ref[tok(c)] = sg[h, l, tok(c)]

    def f(c, k):
        return remote(fs.at[k - 1, tok(c)], fr.at[3 - k, tok(c)], fss.at[k - 1, c], frs.at[3 - k, c], at_y(k))

    def f_recv(c, k):
        return remote(fs.at[3 - k, tok(c)], fr.at[k - 1, tok(c)], fss.at[3 - k, c], frs.at[k - 1, c], at_y(k))

    def project(c):
        n = CHUNKS[c][1]
        for m in (1, 2, 3):
            g_recv(c, m).wait_recv()
        acc[:, tok(c)] = jnp.zeros((4, n, W), F32)

        def body(j, sq):
            v = sg[j // 4, j % 4, tok(c)].astype(F32)
            cols = pl.ds(pl.multiple_of(y * 2048 + j * W, W), W)
            x = (v * gain[:, cols]).astype(BF16)
            mine = pl.ds(pl.multiple_of(j * W, W), W)
            acc[0, tok(c), pl.ds(0, NQ)] += times_t(x, wq0[:, mine])
            for k in (1, 2, 3):
                acc[k, tok(c), pl.ds(0, NQ)] += times_t(x, wq[j, k - 1])
            return sq + jnp.sum(v * v, axis=1, keepdims=True)

        sq = lax.fori_loop(0, 8, body, jnp.zeros((n, 1), F32))
        lane = lax.broadcasted_iota(jnp.int32, (n, W), 1)
        hi = sq.astype(BF16).astype(F32)
        for k in (2, 1, 3):
            v = jnp.where(lane < NQ, acc[k, tok(c)], jnp.where(lane == NQ, hi, sq - hi))
            fs[k - 1, tok(c)] = v.astype(BF16)
            f(c, k).start()
        acc[0, tok(c)] = jnp.where(lane < NQ, acc[0, tok(c)], jnp.where(lane == NQ, hi, sq - hi))

    def finish(c):
        n = CHUNKS[c][1]
        v = acc[0, tok(c)]
        for k in (1, 3, 2):
            f_recv(c, k).wait_recv()
            v = v + fr[k - 1, tok(c)].astype(F32)
        lane = lax.broadcasted_iota(jnp.int32, (n, W), 1)
        extra = jnp.where((lane == NQ) | (lane == NQ + 1), v, 0.0)
        sq = jnp.sum(extra, axis=1, keepdims=True)
        v = v / jnp.sqrt(sq * (1.0 / D) + EPS)
        qkv_ref[tok(c)] = v[:, :NQ].astype(BF16)

    c_hid.wait()
    matmul(2)
    pl.semaphore_wait(barrier, len(peers))
    start(y1(0))
    for k in (2, 1, 3):
        q1(k).start()
    matmul(1)
    y2(0)[0].start()
    matmul(3)
    y2(0)[1].start()
    if NC > 1:
        start(y1(1))
    matmul(0)
    c_wq.wait()
    c_res.wait()
    c_gain.wait()

    def y_step(c):
        aug(c)
        if c == 0:
            for k in (1, 2, 3):
                q1_recv(k).wait_recv()
            for m in (4, 2, 3, 5, 6, 7, 1):
                q2(m).start()
        if c + 1 < NC:
            start(y2(c + 1))
        if c + 2 < NC:
            start(y1(c + 2))
        ysum(c)

    def run(stage, c):
        if stage == 0:
            y_step(c)
        elif stage == 1:
            zsum(c)
        elif stage == 2:
            gather(c)
        elif stage == 3:
            if c == 0:
                for m in range(1, 8):
                    q2_recv(m).wait_recv()
            project(c)
        else:
            finish(c)

    offsets = (0.0, 9.0, 16.0, 25.0, 30.0)
    period = 24.0 / NC
    order = sorted((c * period + offsets[st], st, c) for c in range(NC) for st in range(5))
    for _, st, c in order:
        run(st, c)

    for k in (1, 2, 3):
        q1(k).wait_send()
    for m in range(1, 8):
        q2(m).wait_send()
    for c in range(NC):
        for d in y1(c) + y2(c) + y3(c):
            d.wait_send()
        for m in (1, 2, 3):
            z1(c, m).wait_send()
            g(c, m).wait_send()
            f(c, m).wait_send()
        z2(c).wait_send()


def shards(hidden, down_weight, residual, norm_gain, qkv_weight):
    hbm = pl.BlockSpec(memory_space=pltpu.MemorySpace.HBM)
    vmem = pl.BlockSpec(memory_space=pltpu.VMEM)
    dma = pltpu.SemaphoreType.DMA
    return pl.pallas_call(
        kernel,
        out_shape=(jax.ShapeDtypeStruct((T, W), BF16), jax.ShapeDtypeStruct((T, NQ), BF16)),
        in_specs=[hbm] * 5,
        out_specs=(vmem, vmem),
        scratch_shapes=[
            pltpu.VMEM((T, FG), BF16),
            pltpu.VMEM((4, FG, 2048), BF16),
            pltpu.VMEM((T, W), BF16),
            pltpu.VMEM((1, D), F32),
            pltpu.VMEM((8, 3, NQ, W), BF16),
            pltpu.VMEM((NQ, 2048), BF16),
            pltpu.VMEM((4, 8, T, W), BF16),
            pltpu.VMEM((4, T, W), BF16),
            pltpu.VMEM((4, T, W), BF16),
            pltpu.VMEM((8, T, W), BF16),
            pltpu.VMEM((8, T, W), BF16),
            pltpu.VMEM((2, 4, T, W), BF16),
            pltpu.VMEM((3, 2, T, W), BF16),
            pltpu.VMEM((2, T, W), F32),
            pltpu.VMEM((2, T, W), BF16),
            pltpu.VMEM((2, T, W), BF16),
            pltpu.VMEM((2, 4, T, W), BF16),
            pltpu.VMEM((4, T, W), F32),
            pltpu.VMEM((3, T, W), BF16),
            pltpu.VMEM((3, T, W), BF16),
            dma((4,)), dma((4,)),
            dma((2, NC)), dma((2, NC)), dma((2, NC)), dma((2, NC)), dma((2, NC)), dma((2, NC)),
            dma((3, NC)), dma((3, NC)), dma((NC,)), dma((NC,)),
            dma((3, NC)), dma((3, NC)), dma((3, NC)), dma((3, NC)),
            dma((3,)), dma((3,)), dma((7,)), dma((7,)),
        ],
        compiler_params=pltpu.CompilerParams(
            collective_id=0, has_side_effects=True, vmem_limit_bytes=60 * 1024 * 1024
        ),
        cost_estimate=pl.CostEstimate(flops=1_900_000_000, bytes_accessed=12_000_000, transcendentals=0),
        name="down_norm_qkv",
    )(
        hidden,
        down_weight,
        residual,
        norm_gain.reshape(1, D),
        qkv_weight.T,
    )


def solution(mesh):
    in_specs = (P("dp", "tensor"), P("tensor", None), P("dp", "tensor"), P(), P(None, "tensor"))
    out_specs = (P("dp", "tensor"), P("dp", "tensor"))
    return jax.shard_map(shards, mesh=mesh, in_specs=in_specs, out_specs=out_specs, check_vma=False)
```

```python
import jax
import jax.numpy as jnp
from jax import lax
from jax.experimental import pallas as pl
from jax.experimental.pallas import tpu as pltpu
from jax.sharding import PartitionSpec as P

EPS = 1e-05
T = 192
W = 256
NQ = 160
D = 8192
FG = 448
CHUNKS = ((0, 48), (48, 48), (96, 48), (144, 48))
NC = len(CHUNKS)
GATE_Z = (0, 0, 0, 0)
GATE_G = (1, 0, 0, 0)
ORDER = (
    "A0", "M1", "M3", "B0", "Q1", "Q3", "M0", "A1", "a0", "B1",
    "A2", "Q2", "a1", "y0", "m0", "B2", "A3", "W0", "a2", "y1",
    "m1", "z0", "B3", "a3", "y2", "m2", "z1", "y3", "m3", "g0",
    "z2", "g1", "h0", "z3", "h1", "w0", "p0", "g2", "p1", "g3",
    "h2", "f0", "h3", "p2", "f1", "p3", "f2", "f3",
)
F32 = jnp.float32
BF16 = jnp.bfloat16
MESH = pl.DeviceIdType.MESH


def times_t(a, b):
    return lax.dot_general(a, b, (((1,), (1,)), ((), ())), preferred_element_type=F32)


def kernel(
    hid_hbm, wd_hbm, res_hbm, gain_hbm, wq_hbm,
    stream_ref, qkv_ref,
    hid, wd, res, gain, wq,
    wq0, part, y2a, y2b, y3l, y3r,
    s, zr, agg, aggs, zx, sg, acc, fs, fr,
    lsem, wsem,
    y1s, y1r, y2s, y2r, y3s, y3r_sem,
    z1s, z1r, z2s, z2r, gs, gr, fss, frs,
    q1s, q1r, q2s, q2r,
):
    t = lax.axis_index("tensor")
    dp = lax.axis_index("dp")
    y = t // 8
    z = t % 8
    h = z // 4
    l = z % 4
    rep = dp % 8
    dpb = dp - rep

    def at_y(k):
        return {"tensor": ((y + k) % 4) * 8 + z}

    def quad_l(m):
        lo = l % 2
        hi = l // 2
        if m % 2:
            lo = 1 - lo
        if m // 2:
            hi = 1 - hi
        return hi * 2 + lo

    def at_quad(m):
        return {"tensor": y * 8 + h * 4 + quad_l(m)}

    at_half = {"tensor": y * 8 + (1 - h) * 4 + l}

    def at_rep(m):
        return {"dp": dpb + (rep + m) % 8}

    right, left, across = at_y(1), at_y(3), at_y(2)
    peers = [right, left, across, at_half]
    peers += [at_quad(m) for m in (1, 2, 3)]
    peers += [at_rep(m) for m in range(1, 8)]

    def wd_copy(k):
        col = pl.multiple_of(((y + k) % 4) * 2048, 2048)
        return pltpu.make_async_copy(wd_hbm.at[:, pl.ds(col, 2048)], wd.at[k], wsem.at[k])

    c_hid = pltpu.make_async_copy(hid_hbm, hid, lsem.at[0])
    c_res = pltpu.make_async_copy(res_hbm, res, lsem.at[1])
    c_gain = pltpu.make_async_copy(gain_hbm, gain, lsem.at[2])
    own = pl.multiple_of(y * 2048, 2048)
    c_wq = pltpu.make_async_copy(wq_hbm.at[:, pl.ds(own, 2048)], wq0, lsem.at[3])
    c_hid.start()
    wd_copy(2).start()

    barrier = pltpu.get_barrier_semaphore()
    for p in peers:
        pl.semaphore_signal(barrier, 1, device_id=p, device_id_type=MESH)

    wd_copy(1).start()
    wd_copy(3).start()
    wd_copy(0).start()
    c_wq.start()
    c_res.start()
    c_gain.start()

    def remote(src, dst, ss, rs, dev):
        return pltpu.make_async_remote_copy(
            src_ref=src, dst_ref=dst, send_sem=ss, recv_sem=rs, device_id=dev, device_id_type=MESH
        )

    def matmul(k):
        wd_copy(k).wait()

        for half in range(2):
            v = jnp.dot(hid[...], wd[k, :, half * 1024:half * 1024 + 1024], preferred_element_type=F32)
            for j in range(4):
                part[k, half * 4 + j] = v[:, j * W:(j + 1) * W].astype(BF16)

    def tok(c):
        return pl.ds(CHUNKS[c][0], CHUNKS[c][1])

    LO, HI = pl.ds(0, 4), pl.ds(4, 4)

    def wq_cols(owner):
        return pl.ds(pl.multiple_of(owner * 2048 + rep * W, W), W)

    def q1(k):
        src = wq_hbm.at[:, wq_cols((y + k) % 4)]
        return remote(src, wq.at[rep, 3 - k], q1s.at[k - 1], q1r.at[3 - k], at_y(k))

    def q1_recv(k):
        src = wq_hbm.at[:, wq_cols(y)]
        return remote(src, wq.at[rep, k - 1], q1s.at[3 - k], q1r.at[k - 1], at_y(k))

    def q2(m):
        blk = wq.at[rep]
        return remote(blk, blk, q2s.at[m - 1], q2r.at[m - 1], at_rep(m))

    def q2_recv(m):
        blk = wq.at[(rep + 8 - m) % 8]
        return remote(blk, blk, q2s.at[m - 1], q2r.at[m - 1], at_rep(m))

    def y1(c):
        return (
            remote(part.at[2, LO, tok(c)], y2a.at[:, tok(c)], y1s.at[0, c], y1r.at[0, c], right),
            remote(part.at[2, HI, tok(c)], y2b.at[:, tok(c)], y1s.at[1, c], y1r.at[1, c], left),
        )

    def y2(c):
        return (
            remote(part.at[1, HI, tok(c)], y3l.at[HI, tok(c)], y2s.at[0, c], y2r.at[0, c], right),
            remote(part.at[3, LO, tok(c)], y3r.at[LO, tok(c)], y2s.at[1, c], y2r.at[1, c], left),
        )

    def y3(c):
        return (
            remote(y2a.at[:, tok(c)], y3l.at[LO, tok(c)], y3s.at[0, c], y3r_sem.at[0, c], right),
            remote(y2b.at[:, tok(c)], y3r.at[HI, tok(c)], y3s.at[1, c], y3r_sem.at[1, c], left),
        )

    def start(ds):
        for d in ds:
            d.start()

    def aug(c):
        ra, rb = y1(c)
        ra.wait_recv()

        def body_a(j, x):
            y2a[j, tok(c)] = (y2a[j, tok(c)].astype(F32) + part[1, j, tok(c)].astype(F32)).astype(BF16)
            return x

        lax.fori_loop(0, 4, body_a, 0)
        y3(c)[0].start()
        rb.wait_recv()

        def body_b(j, x):
            y2b[j, tok(c)] = (y2b[j, tok(c)].astype(F32) + part[3, 4 + j, tok(c)].astype(F32)).astype(BF16)
            return x

        lax.fori_loop(0, 4, body_b, 0)
        y3(c)[1].start()

    inner = (l == 1) | (l == 2)
    outer = (l == 0) | (l == 3)
    low = l < 2
    mate = quad_l(1)
    far_in = jnp.where(low, 2, 1)
    far_out = jnp.where(low, 3, 0)
    at_mate = at_quad(1)
    at_far_in = {"tensor": y * 8 + h * 4 + far_in}
    at_far_out = {"tensor": y * 8 + h * 4 + far_out}
    own_slot = jnp.where(l == 2, 2, 0)

    def slot_of(piece):
        return jnp.where(low, piece - 1, piece)

    def z1(c, m):
        dst = quad_l(m)
        return remote(s.at[:, dst, tok(c)], zr.at[:, m - 1, tok(c)], z1s.at[m - 1, c], z1r.at[m - 1, c], at_quad(m))

    def z1_outer(c):
        src = s.at[:, pl.ds(jnp.where(l == 0, 1, 0), 3), tok(c)]
        return remote(src, zr.at[:, pl.ds(0, 3), tok(c)], z1s.at[0, c], z1r.at[0, c], at_mate)

    def z1_inner(c):
        return remote(s.at[:, mate, tok(c)], zr.at[:, 0, tok(c)], z1s.at[0, c], z1r.at[0, c], at_mate)

    def z1_merged(c):
        return (
            remote(s.at[:, far_out, tok(c)], zr.at[:, 3, tok(c)], z1s.at[1, c], z1r.at[1, c], at_far_out),
            remote(s.at[:, far_in, tok(c)], zr.at[:, 3, tok(c)], z1s.at[2, c], z1r.at[1, c], at_far_in),
        )

    def merge(c):
        if not GATE_Z[c]:
            return

        @pl.when(inner)
        def _():
            z1_outer(c).wait_recv()
            for piece, copy in zip((far_out, far_in), z1_merged(c)):
                for hh in range(2):
                    v = s[hh, piece, tok(c)].astype(F32) + zr[hh, slot_of(piece), tok(c)].astype(F32)
                    s[hh, piece, tok(c)] = v.astype(BF16)
                copy.start()

    def ysum(c):
        for d in y2(c) + y3(c):
            d.wait_recv()

        def body(j, x):
            v = part[0, j, tok(c)].astype(F32) + y3l[j, tok(c)].astype(F32) + y3r[j, tok(c)].astype(F32)
            s[j // 4, j % 4, tok(c)] = v.astype(BF16)
            return x

        lax.fori_loop(0, 8, body, 0)
        if GATE_Z[c]:
            pl.when(outer)(lambda: z1_outer(c).start())
            pl.when(inner)(lambda: z1_inner(c).start())
        else:
            for m in (3, 2, 1):
                z1(c, m).start()

    def z2(c):
        return remote(aggs.at[:, tok(c)], zx.at[:, tok(c)], z2s.at[c], z2r.at[c], at_half)

    def zsum(c):
        if c == 0:
            c_res.wait()
        if GATE_Z[c]:
            pl.when(outer)(lambda: z1_inner(c).wait_recv())
            z1_merged(c)[0].wait_recv()
        else:
            for m in (1, 2, 3):
                z1(c, m).wait_recv()

        def body(hh, x):
            v = s[hh, l, tok(c)].astype(F32)
            if GATE_Z[c]:
                v = v + zr[hh, own_slot, tok(c)].astype(F32) + zr[hh, 3, tok(c)].astype(F32)
            else:
                for m in range(3):
                    v = v + zr[hh, m, tok(c)].astype(F32)
            mine = jnp.where(hh == h, 1.0, 0.0).astype(F32)
            v = v + res[tok(c)].astype(F32) * mine
            agg[hh, tok(c)] = v
            aggs[hh, tok(c)] = v.astype(BF16)
            return x

        lax.fori_loop(0, 2, body, 0)
        z2(c).start()

    def g(c, i, piece, dev):
        blk = sg.at[:, piece, tok(c)]
        return remote(blk, blk, gs.at[i, c], gr.at[piece, c], dev)

    def g_own(c):
        if GATE_G[c]:
            return (g(c, 0, l, at_far_in), g(c, 1, l, at_mate))
        return tuple(g(c, m - 1, l, at_quad(m)) for m in (3, 2, 1))

    def g_pass(c):
        return (g(c, 2, far_in, at_mate), g(c, 3, far_out, at_mate))

    def g_in(c, piece):
        return g(c, 0, piece, at_mate)

    def hand_on(c):
        if not GATE_G[c]:
            return

        @pl.when(inner)
        def _():
            for piece, copy in zip((far_in, far_out), g_pass(c)):
                g_in(c, piece).wait_recv()
                copy.start()

    def gather(c):
        z2(c).wait_recv()

        def body(hh, x):
            v = agg[hh, tok(c)] + zx[hh, tok(c)].astype(F32)
            sg[hh, l, tok(c)] = v.astype(BF16)
            return x

        lax.fori_loop(0, 2, body, 0)
        start(g_own(c))
        stream_ref[tok(c)] = sg[h, l, tok(c)]

    def f(c, k):
        return remote(fs.at[k - 1, tok(c)], fr.at[3 - k, tok(c)], fss.at[k - 1, c], frs.at[3 - k, c], at_y(k))

    def f_recv(c, k):
        return remote(fs.at[3 - k, tok(c)], fr.at[k - 1, tok(c)], fss.at[3 - k, c], frs.at[k - 1, c], at_y(k))

    def project(c):
        n = CHUNKS[c][1]
        if GATE_G[c]:
            g_in(c, mate).wait_recv()

            @pl.when(outer)
            def _():
                for piece in (far_in, far_out):
                    g_in(c, piece).wait_recv()
        else:
            for m in (1, 2, 3):
                g_in(c, quad_l(m)).wait_recv()

        acc[:, tok(c)] = jnp.zeros((4, n, W), F32)

        def body(j, sq):
            v = sg[j // 4, j % 4, tok(c)].astype(F32)
            cols = pl.ds(pl.multiple_of(y * 2048 + j * W, W), W)
            x = (v * gain[:, cols]).astype(BF16)
            mine = pl.ds(pl.multiple_of(j * W, W), W)
            acc[0, tok(c), pl.ds(0, NQ)] += times_t(x, wq0[:, mine])
            for k in (1, 2, 3):
                acc[k, tok(c), pl.ds(0, NQ)] += times_t(x, wq[j, k - 1])
            return sq + jnp.sum(v * v, axis=1, keepdims=True)

        sq = lax.fori_loop(0, 8, body, jnp.zeros((n, 1), F32))
        lane = lax.broadcasted_iota(jnp.int32, (n, W), 1)
        hi = sq.astype(BF16).astype(F32)
        for k in (2, 1, 3):
            v = jnp.where(lane < NQ, acc[k, tok(c)], jnp.where(lane == NQ, hi, sq - hi))
            fs[k - 1, tok(c)] = v.astype(BF16)
            f(c, k).start()
        acc[0, tok(c)] = jnp.where(lane < NQ, acc[0, tok(c)], jnp.where(lane == NQ, hi, sq - hi))

    def finish(c):
        n = CHUNKS[c][1]
        v = acc[0, tok(c)]
        for k in (1, 3, 2):
            f_recv(c, k).wait_recv()
            v = v + fr[k - 1, tok(c)].astype(F32)
        lane = lax.broadcasted_iota(jnp.int32, (n, W), 1)
        extra = jnp.where((lane == NQ) | (lane == NQ + 1), v, 0.0)
        sq = jnp.sum(extra, axis=1, keepdims=True)
        v = v / jnp.sqrt(sq * (1.0 / D) + EPS)
        qkv_ref[tok(c)] = v

    def weights_out(k):
        q1(k).start()

    def weights_on(c):
        for k in (1, 2, 3):
            q1_recv(k).wait_recv()
        for m in (4, 2, 3, 5, 6, 7, 1):
            q2(m).start()

    def weights_in(c):
        c_wq.wait()
        c_gain.wait()
        for m in range(1, 8):
            q2_recv(m).wait_recv()

    def first(c):
        start(y1(c))

    def plain(c):
        start(y2(c))

    c_hid.wait()
    matmul(2)
    pl.semaphore_wait(barrier, len(peers))
    steps = {
        "A": first, "B": plain, "M": matmul, "Q": weights_out, "W": weights_on, "w": weights_in,
        "a": aug, "y": ysum, "z": zsum, "g": gather, "p": project, "f": finish,
        "m": merge, "h": hand_on,
    }
    for step in ORDER:
        steps[step[0]](int(step[1]))

    for k in (1, 2, 3):
        q1(k).wait_send()
    for m in range(1, 8):
        q2(m).wait_send()
    for c in range(NC):
        for d in y1(c) + y2(c) + y3(c):
            d.wait_send()
        if GATE_Z[c]:
            pl.when(outer)(lambda: z1_outer(c).wait_send())

            @pl.when(inner)
            def _():
                z1_inner(c).wait_send()
                for d in z1_merged(c):
                    d.wait_send()
        else:
            for m in (1, 2, 3):
                z1(c, m).wait_send()
        for d in g_own(c):
            d.wait_send()
        if GATE_G[c]:

            @pl.when(inner)
            def _():
                for d in g_pass(c):
                    d.wait_send()
        for m in (1, 2, 3):
            f(c, m).wait_send()
        z2(c).wait_send()


def place(stream_in, qkv_in, stream_out, qkv_out, turned, sem):
    a = pltpu.make_async_copy(stream_in, stream_out, sem.at[0])
    a.start()
    turned[...] = jnp.transpose(qkv_in[...])[:NQ].astype(BF16)
    b = pltpu.make_async_copy(turned, qkv_out, sem.at[1])
    b.start()
    a.wait()
    b.wait()


def shards(hidden, down_weight, residual, norm_gain, qkv_weight):
    hbm = pl.BlockSpec(memory_space=pltpu.MemorySpace.HBM)
    vmem = pl.BlockSpec(memory_space=pltpu.VMEM)
    dma = pltpu.SemaphoreType.DMA
    stream, qkv = pl.pallas_call(
        kernel,
        out_shape=(jax.ShapeDtypeStruct((T, W), BF16), jax.ShapeDtypeStruct((T, W), F32)),
        in_specs=[hbm] * 5,
        out_specs=(vmem, vmem),
        scratch_shapes=[
            pltpu.VMEM((T, FG), BF16),
            pltpu.VMEM((4, FG, 2048), BF16),
            pltpu.VMEM((T, W), BF16),
            pltpu.VMEM((1, D), F32),
            pltpu.VMEM((8, 3, NQ, W), BF16),
            pltpu.VMEM((NQ, 2048), BF16),
            pltpu.VMEM((4, 8, T, W), BF16),
            pltpu.VMEM((4, T, W), BF16),
            pltpu.VMEM((4, T, W), BF16),
            pltpu.VMEM((8, T, W), BF16),
            pltpu.VMEM((8, T, W), BF16),
            pltpu.VMEM((2, 4, T, W), BF16),
            pltpu.VMEM((2, 4, T, W), BF16),
            pltpu.VMEM((2, T, W), F32),
            pltpu.VMEM((2, T, W), BF16),
            pltpu.VMEM((2, T, W), BF16),
            pltpu.VMEM((2, 4, T, W), BF16),
            pltpu.VMEM((4, T, W), F32),
            pltpu.VMEM((3, T, W), BF16),
            pltpu.VMEM((3, T, W), BF16),
            dma((4,)), dma((4,)),
            dma((2, NC)), dma((2, NC)), dma((2, NC)), dma((2, NC)), dma((2, NC)), dma((2, NC)),
            dma((3, NC)), dma((3, NC)), dma((NC,)), dma((NC,)),
            dma((4, NC)), dma((4, NC)), dma((3, NC)), dma((3, NC)),
            dma((3,)), dma((3,)), dma((7,)), dma((7,)),
        ],
        compiler_params=pltpu.CompilerParams(
            collective_id=0, has_side_effects=True, vmem_limit_bytes=60 * 1024 * 1024
        ),
        cost_estimate=pl.CostEstimate(flops=1_900_000_000, bytes_accessed=12_000_000, transcendentals=0),
        name="down_norm_qkv",
    )(
        hidden,
        down_weight,
        residual,
        norm_gain.reshape(1, D),
        qkv_weight.T,
    )
    stream, qkv_t = pl.pallas_call(
        place,
        out_shape=(jax.ShapeDtypeStruct((T, W), BF16), jax.ShapeDtypeStruct((NQ, T), BF16)),
        in_specs=[vmem, vmem],
        out_specs=(hbm, hbm),
        scratch_shapes=[pltpu.VMEM((NQ, T), BF16), dma((2,))],
        name="place",
    )(stream, qkv)
    return (stream, qkv_t.T)


def solution(mesh):
    in_specs = (P("dp", "tensor"), P("tensor", None), P("dp", "tensor"), P(), P(None, "tensor"))
    out_specs = (P("dp", "tensor"), P("dp", "tensor"))
    return jax.shard_map(shards, mesh=mesh, in_specs=in_specs, out_specs=out_specs, check_vma=False)
```
